256 devices in a mesh: cent: 16 (over y, z_lo), pts: 16 (over x, z_hi, core).
Axes of the slice: x: 4, y: 4, z: 8 (z_hi: 2, z_lo: 4; z = z_hi * 4 + z_lo), core: 2. Of those that a mesh axis runs over, the one named last changes fastest.
Arguments:
- points: bfloat16 [32768, 1024], P('pts'), may hold values from -30 to 30
- center_one: bfloat16 [16384, 1024], P('cent'), may hold values from -9 to 9
- center_two: bfloat16 [4096, 1024], P('pts'), may hold values from -28 to 28
Outputs:
- level_one: bfloat16 [16384, 1024], P(('cent', 'pts'))
- level_two: bfloat16 [4096, 1024], P('pts')
The draws below stay inside these ranges and needn't reach their ends.
All inputs are finite; a program needn't handle non-finite values.
Results may differ from the reference program's by a relative error of at most 0.0051.
Values may be sent and summed in bfloat16 or wider, within the bound.
No kernel may reach another device: no remote copies, remote signals or barrier semaphores. Data moves between devices by JAX's collectives and lax.ppermute only.
A program may use at most 64 MiB of HBM per device.

```python
import jax
import jax.numpy as jnp
from jax import lax

D = 1024
P_DEV = 2048
K1_DEV = 1024
K2 = 4096
POINTS = 32768
K1 = 16384


def shared_layout(key):
    anchor = jax.random.truncated_normal(jax.random.fold_in(key, 11), -6.0, 6.0, (K1, D), jnp.float32)
    return anchor


def draw_points(key, part):
    key = jax.random.fold_in(key, 2)
    values = jax.random.truncated_normal(key, -6.0, 6.0, (POINTS, D), jnp.float32)
    return values.astype(jnp.bfloat16)


def draw_center_one(key, part):
    anchor = shared_layout(key)
    values = anchor
    return values.astype(jnp.bfloat16)


def draw_center_two(key, part):
    key = jax.random.fold_in(key, 3)
    values = jax.random.truncated_normal(key, -6.0, 6.0, (K2, D), jnp.float32)
    return values.astype(jnp.bfloat16)


def setup_inputs(seed: int = 0) -> dict:
    streams_of = jax.random.split(jax.random.key(seed), 4)
    points = draw_points(jax.random.fold_in(streams_of[3], 71), 0)
    center_one = draw_center_one(jax.random.fold_in(streams_of[3], 71), 0)
    center_two = draw_center_two(jax.random.fold_in(streams_of[3], 71), 0)
    return dict(points=points, center_one=center_one, center_two=center_two)


sharpness_coefficient = 100.0

def normalize_rows(values):
    return (values * lax.rsqrt(lax.optimization_barrier(jnp.mean(values * values, axis=1, keepdims=True)) + 1e-05)).astype(jnp.bfloat16)

def soft_sums(queries, centers, block):
    embedding_dimension = queries.shape[1]
    normalizing_multiplier = sharpness_coefficient / embedding_dimension
    blocks = queries.reshape(queries.shape[0] // block, block, embedding_dimension)

    def advance(accum, segment):
        logits = jnp.dot(segment, centers.T, preferred_element_type=jnp.float32) * normalizing_multiplier
        peak = lax.optimization_barrier(jnp.max(logits, axis=1, keepdims=True))
        powers = jnp.exp(logits - peak)
        aggregate_masses = lax.optimization_barrier(jnp.sum(powers, axis=1, keepdims=True))
        weights = (powers / aggregate_masses).astype(jnp.bfloat16)
        added = lax.dot_general(weights, segment, (((0,), (0,)), ((), ())), preferred_element_type=jnp.float32)
        return (accum + added, None)
    accum, discarded_output = lax.scan(advance, jnp.zeros((centers.shape[0], embedding_dimension), jnp.float32), blocks)
    return accum

def reference(points, center_one, center_two):
    level_one = normalize_rows(soft_sums(points, center_one, P_DEV) + center_one.astype(jnp.float32))
    level_two = normalize_rows(soft_sums(level_one, center_two, K1_DEV) + center_two.astype(jnp.float32))
    return (level_one, level_two)
```

```python
import jax
import jax.numpy as jnp
from jax import lax
from jax.sharding import Mesh
from jax.sharding import PartitionSpec as P

sharpness_coefficient = 100.0
AXES = ("y", "zl", "x", "zh", "core")


def shifted(value, axis, step):
    size = lax.axis_size(axis)
    return lax.ppermute(value, axis, [(i, (i + step) % size) for i in range(size)])


def from_others(value, axis):
    return [shifted(value, axis, k) for k in range(1, lax.axis_size(axis))]


def merge(parts):
    peak = parts[0][0]
    for part in parts[1:]:
        peak = jnp.maximum(peak, part[0])
    total = sum(part[1] * jnp.exp(part[0] - peak) for part in parts)
    return jnp.stack([peak, total])


def normalize_rows(values):
    return (values * lax.rsqrt(jnp.mean(values * values, axis=-1, keepdims=True) + 1e-05)).astype(
        jnp.bfloat16
    )


def logits_of(centers, rows, scale):
    return (
        lax.dot_general(centers, rows, (((1,), (1,)), ((), ())), preferred_element_type=jnp.float32)
        * scale
    )


def softmax_parts(logits):
    peak = jnp.max(logits, axis=0)
    powers = jnp.exp(logits - peak[None, :])
    return powers, jnp.stack([peak, jnp.sum(powers, axis=0)])


def rescale(local, whole):
    return jnp.exp(local[0] - whole[0]) / whole[1]


def reduce_scatter(blocks, axis):
    size = lax.axis_size(axis)
    me = lax.axis_index(axis)
    take = lambda i: lax.dynamic_index_in_dim(blocks, lax.rem(i, size), 0, keepdims=False)
    got = [shifted(take(me + k).astype(jnp.bfloat16), axis, k) for k in range(1, size)]
    total = take(me)
    for part in got:
        total = total + part.astype(jnp.float32)
    return total


def shards(points, center_one, center_two):
    depth = points.shape[1]
    scale = sharpness_coefficient / depth
    nx, nh, nc = lax.axis_size("x"), lax.axis_size("zh"), lax.axis_size("core")
    ix, ih, ic = lax.axis_index("x"), lax.axis_index("zh"), lax.axis_index("core")
    held = center_one.shape[0]
    owned = held // (nx * nh * nc)

    some_two = jnp.concatenate([center_two] + from_others(center_two, "x"))
    some_two = jnp.concatenate([some_two] + from_others(some_two, "core"))

    powers, local = softmax_parts(logits_of(center_one, points, scale))
    whole = merge([local] + from_others(local, "y"))
    whole = merge([whole] + from_others(whole, "zl"))
    weight = (powers * rescale(local, whole)[None, :]).astype(jnp.bfloat16)
    sums = jnp.dot(weight, points, preferred_element_type=jnp.float32)
    sums = sums.reshape(nx, nh, nc, owned, depth)

    part = reduce_scatter(jnp.moveaxis(sums, 2, 0), "core")
    part = reduce_scatter(part, "x")
    other = shifted(part.astype(jnp.bfloat16), "zh", 1)
    mine = center_one.reshape(nx, nh, nc, owned, depth)
    mine = lax.dynamic_index_in_dim(mine, ic, 2, keepdims=False)
    mine = lax.dynamic_index_in_dim(mine, ix, 0, keepdims=False)
    rows = normalize_rows(part + other.astype(jnp.float32) + mine.astype(jnp.float32))
    level_one = lax.dynamic_index_in_dim(rows, ih, 0, keepdims=False)
    rows = rows.reshape(nh * owned, depth)

    _, own = softmax_parts(logits_of(some_two, rows, scale))
    own = merge([own, shifted(own, "zh", 1)])
    own = jnp.concatenate([own] + from_others(own, "x"), axis=1)
    whole_two = jnp.concatenate([own] + from_others(own, "core"), axis=1)

    rows = jnp.concatenate([rows] + from_others(rows, "x"))
    rows = jnp.concatenate([rows] + from_others(rows, "core"))
    logits = logits_of(center_two, rows, scale)
    weight = (jnp.exp(logits - whole_two[0][None, :]) * (1.0 / whole_two[1])[None, :]).astype(jnp.bfloat16)
    sums = jnp.dot(weight, rows, preferred_element_type=jnp.float32)

    ny, nl = lax.axis_size("y"), lax.axis_size("zl")
    iy, il = lax.axis_index("y"), lax.axis_index("zl")
    sums = sums.reshape(ny, nl, -1, depth)
    part = reduce_scatter(reduce_scatter(sums, "y"), "zl")
    mine = center_two.reshape(ny, nl, -1, depth)
    mine = lax.dynamic_index_in_dim(mine, iy, 0, keepdims=False)
    mine = lax.dynamic_index_in_dim(mine, il, 0, keepdims=False)
    done = normalize_rows(part + mine.astype(jnp.float32))
    for axis in ("zl", "y"):
        size, me = lax.axis_size(axis), lax.axis_index(axis)
        parts = jnp.stack([done] + from_others(done, axis))
        order = lax.rem(me - jnp.arange(size) + size, size)
        done = jnp.take(parts, order, axis=0)
        done = done.reshape((-1,) + done.shape[2:])
    return level_one, done


def solution(mesh):
    fine = Mesh(mesh.devices.reshape(4, 4, 4, 2, 2), AXES)
    cent, pts = ("y", "zl"), ("x", "zh", "core")
    in_specs = (P(pts, None), P(cent, None), P(pts, None))
    out_specs = (P(cent + pts, None), P(pts, None))
    return jax.shard_map(shards, mesh=fine, in_specs=in_specs, out_specs=out_specs, check_vma=False)
```

```python
import functools

import jax
import jax.numpy as jnp
from jax import lax
from jax.experimental import pallas as pl
from jax.experimental.pallas import tpu as pltpu
from jax.sharding import Mesh
from jax.sharding import PartitionSpec as P

sharpness_coefficient = 100.0
AXES = ("y", "zl", "x", "zh", "core")
MIB = 1024 * 1024
VMEM = pl.BlockSpec(memory_space=pltpu.VMEM)
HBM = pl.BlockSpec(memory_space=pltpu.HBM)

def swapped(value, axis, mask=1):
    return lax.ppermute(value, axis, [(i, i ^ mask) for i in range(lax.axis_size(axis))])


def from_others(value, axis):
    return [swapped(value, axis, k) for k in range(1, lax.axis_size(axis))]


def kernel_call(body, name, flops, in_specs, out_specs, out_shape, vmem=12, **more):
    return pl.pallas_call(
        body,
        in_specs=in_specs,
        out_specs=out_specs,
        out_shape=out_shape,
        compiler_params=pltpu.CompilerParams(vmem_limit_bytes=vmem * MIB),
        cost_estimate=pl.CostEstimate(flops=flops, bytes_accessed=1024, transcendentals=0),
        name=name,
        **more,
    )


def f32(value):
    return value.astype(jnp.float32)


def bf16(value):
    return value.astype(jnp.bfloat16)


def shape(dims, dtype=jnp.bfloat16):
    return jax.ShapeDtypeStruct(dims, dtype)


def times_rows(left, right):
    return lax.dot_general(left, right, (((1,), (1,)), ((), ())), preferred_element_type=jnp.float32)


def merge(parts):
    peak = functools.reduce(jnp.maximum, [part[0:1] for part in parts])
    return peak, sum(part[1:2] * jnp.exp(part[0:1] - peak) for part in parts)


def normalize(values):
    return bf16(values * lax.rsqrt(jnp.mean(values * values, axis=-1, keepdims=True) + 1e-05))


def merge_kernel(count, *refs):
    peak, total = merge([ref[...] for ref in refs[:count]])
    refs[-1][0:1, :] = peak
    refs[-1][1:2, :] = total


def merge_stats(parts):
    return kernel_call(
        functools.partial(merge_kernel, len(parts)),
        "merge_stats",
        1_000_000,
        [VMEM] * len(parts),
        VMEM,
        shape(parts[0].shape, jnp.float32),
    )(*parts)


def powers_kernel(scale, step, center_ref, point_ref, power_ref, stat_ref):
    for start in range(0, point_ref.shape[0], step):
        columns = slice(start, start + step)
        raw = times_rows(center_ref[...], point_ref[columns, :])
        peak = jnp.max(raw, axis=0, keepdims=True)
        powers = jnp.exp((raw - peak) * scale)
        stat_ref[0:1, columns] = peak * scale
        stat_ref[1:2, columns] = jnp.sum(powers, axis=0, keepdims=True)
        power_ref[:, columns] = bf16(powers)


def level_one_powers(center, points, scale):
    held, depth = center.shape
    count = points.shape[0]
    return kernel_call(
        functools.partial(powers_kernel, scale, 512),
        "level_one_powers",
        2 * held * count * depth,
        [VMEM] * 2,
        [VMEM] * 2,
        [shape((held, count)), shape((2, count), jnp.float32)],
        vmem=20,
    )(center, points)


def sums_kernel(near, other_core, local_ref, *refs):
    stat_refs, power_ref, point_ref, out_ref = refs[:near], refs[near], refs[near + 1], refs[-1]
    nx, nh, _, owned, count = power_ref.shape
    peak, total = merge([ref[...] for ref in stat_refs])
    factor = jnp.exp(local_ref[0:1, :] - peak) / total
    core = lax.axis_index("core") ^ int(other_core)
    for k in range(nx):
        powers = power_ref[lax.axis_index("x") ^ k, :, core].reshape(nh * owned, count)
        weight = bf16(f32(powers) * factor)
        sums = jnp.dot(weight, point_ref[...], preferred_element_type=jnp.float32)
        out_ref[k] = sums.astype(out_ref.dtype).reshape(nh, owned, -1)


def level_one_sums(other_core, local, stats, powers, points, dtype):
    nx, nh, _, owned, count = powers.shape
    depth = points.shape[1]
    return kernel_call(
        functools.partial(sums_kernel, len(stats), other_core),
        "level_one_sums",
        2 * nx * nh * owned * count * depth,
        [VMEM] * (3 + len(stats)),
        VMEM,
        shape((nx, nh, owned, depth), dtype),
    )(local, *stats, powers, points)


def split_kernel(parts, kept_ref, got_ref, *refs):
    size = kept_ref.shape[0]
    for part in range(parts):
        hold_ref, *send_refs = refs[part * size : (part + 1) * size]
        hold_ref[...] = kept_ref[0, part] + f32(got_ref[0, part])
        for k, send_ref in enumerate(send_refs, 1):
            send_ref[...] = bf16(kept_ref[k, part] + f32(got_ref[k, part]))


def total_kernel(hold_ref, *refs):
    refs[-1][...] = bf16(hold_ref[...] + sum(f32(ref[...]) for ref in refs[:-1]))


def axis_sums(kept, got, axis):
    size, parts, *block = kept.shape
    outs = kernel_call(
        functools.partial(split_kernel, parts),
        "split",
        1_000_000,
        [VMEM] * 2,
        [VMEM] * (size * parts),
        ([shape(block, jnp.float32)] + [shape(block)] * (size - 1)) * parts,
    )(kept, got)
    sums = []
    for part in range(parts):
        hold, *sends = outs[part * size : (part + 1) * size]
        arrived = [swapped(send, axis, k) for k, send in enumerate(sends, 1)]
        sums.append(
            kernel_call(total_kernel, "total", 1_000_000, [VMEM] * size, VMEM, shape(block))(hold, *arrived)
        )
    return sums


def rows_kernel(half, part_ref, other_ref, center_hbm, row_ref, center_ref, sem):
    mine = center_hbm.at[lax.axis_index("x"), half, lax.axis_index("core")]
    copy = pltpu.make_async_copy(mine, center_ref, sem)
    copy.start()
    copy.wait()
    row_ref[...] = normalize(f32(part_ref[...]) + f32(other_ref[...]) + f32(center_ref[...]))


def new_rows(half, part, other, centers):
    return kernel_call(
        functools.partial(rows_kernel, half),
        "new_rows",
        1_000_000,
        [VMEM] * 2 + [HBM],
        VMEM,
        shape(part.shape),
        scratch_shapes=[pltpu.VMEM(part.shape, jnp.bfloat16), pltpu.SemaphoreType.DMA],
    )(part, other, centers)


def own_kernel(a_ref, b_ref, out_ref):
    out_ref[...] = jnp.where(lax.axis_index("zh") == 0, a_ref[...], b_ref[...])


def own_rows(a, b):
    return kernel_call(own_kernel, "own_rows", 1_000_000, [VMEM] * 2, VMEM, shape(a.shape))(a, b)


def powers_two_kernel(scale, ny, own_ref, other_ref, *refs):
    piece_refs, (row_ref, power_ref, stat_ref, center_ref) = refs[:-4], refs[-4:]
    held = own_ref.shape[0]
    block = held // ny
    for core, ref in enumerate((own_ref, other_ref)):
        for k in range(ny):
            place = pl.ds(pl.multiple_of((lax.axis_index("y") ^ k) * block, block), block)
            center_ref[core * held + k * block : core * held + (k + 1) * block, :] = ref[place, :]
    around = lax.axis_size("x")
    for i, ref in enumerate(piece_refs):
        size = ref.shape[0]
        first = (lax.axis_index("x") ^ (i % around)) * size + (i // around) * around * size
        row_ref[pl.ds(pl.multiple_of(first, size), size), :] = ref[...]
    raw = times_rows(center_ref[...], row_ref[...])
    peak = jnp.max(raw, axis=0, keepdims=True)
    powers = jnp.exp((raw - peak) * scale)
    stat_ref[0:1, :] = peak * scale
    stat_ref[1:2, :] = jnp.sum(powers, axis=0, keepdims=True)
    power_ref[...] = bf16(powers)


def level_two_powers(own, other, pieces, ny, scale):
    held, depth = own.shape
    count = sum(p.shape[0] for p in pieces)
    return kernel_call(
        functools.partial(powers_two_kernel, scale, ny),
        "level_two_powers",
        4 * held * count * depth,
        [VMEM] * (2 + len(pieces)),
        [VMEM] * 3,
        [shape((count, depth)), shape((2 * held, count)), shape((2, count), jnp.float32)],
        scratch_shapes=[pltpu.VMEM((2 * held, depth), jnp.bfloat16)],
    )(own, other, *pieces)


def sums_two_kernel(first, local_ref, power_ref, row_ref, *refs):
    stat_refs, out_ref = refs[:-1], refs[-1]
    peak, total = merge([ref[...] for ref in stat_refs])
    factor = jnp.exp(local_ref[0:1, :] - peak) / total
    held = power_ref.shape[0] // 2
    weight = bf16(f32(power_ref[first : first + held, :]) * factor)
    sums = jnp.dot(weight, row_ref[...], preferred_element_type=jnp.float32)
    out_ref[...] = sums.astype(out_ref.dtype).reshape(out_ref.shape)


def level_two_sums(other_core, local, stats, powers, rows, ny, dtype):
    held = powers.shape[0] // 2
    count, depth = rows.shape
    return kernel_call(
        functools.partial(sums_two_kernel, held if other_core else 0),
        "level_two_sums",
        2 * held * count * depth,
        [VMEM] * (3 + len(stats)),
        VMEM,
        shape((ny, 1, held // ny, depth), dtype),
    )(local, powers, rows, *stats)


def finish_kernel(center_ref, a_ref, b_ref, c_ref, d_ref, out_ref):
    size = a_ref.shape[0]
    values = (f32(a_ref[...]) + f32(b_ref[...])) + (f32(c_ref[...]) + f32(d_ref[...]))
    start = pl.multiple_of(lax.axis_index("y") * size, size)
    out_ref[...] = normalize(values + f32(center_ref[pl.ds(start, size), :]))


def finish(center, parts):
    return kernel_call(
        finish_kernel, "finish", 1_000_000, [VMEM] * 5, VMEM, shape(parts[0].shape)
    )(center, *parts)


def place_kernel(*refs):
    block_refs, out_ref, sems = refs[:-2], refs[-2], refs[-1]
    size = block_refs[0].shape[0]
    copies = []
    for k, ref in enumerate(block_refs):
        rows = pl.ds(pl.multiple_of((lax.axis_index("y") ^ k) * size, size), size)
        copies.append(pltpu.make_async_copy(ref, out_ref.at[rows, :], sems.at[k]))
    for copy in copies:
        copy.start()
    for copy in copies:
        copy.wait()


def place(blocks, like):
    return kernel_call(
        place_kernel,
        "place",
        1_000_000,
        [VMEM] * len(blocks),
        HBM,
        shape(like.shape),
        scratch_shapes=[pltpu.SemaphoreType.DMA((len(blocks),))],
    )(*blocks)


def shards(points, center_one, center_two):
    held, depth = center_one.shape
    scale = sharpness_coefficient / depth
    ny, nl, nx, nh, nc = (lax.axis_size(a) for a in AXES)
    owned = held // (nx * nh * nc)

    powers, local = level_one_powers(center_one, points, scale)
    near = merge_stats([local] + from_others(local, "y"))
    powers = powers.reshape(nx, nh, nc, owned, -1)
    stats = [near] + from_others(near, "zl")
    sent = level_one_sums(True, local, stats, powers, points, jnp.bfloat16)
    got = swapped(sent, "core")
    kept = level_one_sums(False, local, stats, powers, points, jnp.float32)

    centers = center_one.reshape(nx, nh, nc, owned, depth)
    rows = []
    for half, part in enumerate(axis_sums(kept, got, "x")):
        rows.append(new_rows(half, part, swapped(part, "zh"), centers))
    level_one = own_rows(*rows)

    two_core = swapped(center_two, "core")
    pieces = [piece for half in rows for piece in [half] + from_others(half, "x")]
    rows, powers, local = level_two_powers(center_two, two_core, pieces, ny, scale)
    near = merge_stats([local] + from_others(local, "x"))
    stats = [near, swapped(near, "zh")]
    sent = level_two_sums(True, local, stats, powers, rows, ny, jnp.bfloat16)
    got = swapped(sent, "core")
    kept = level_two_sums(False, local, stats, powers, rows, ny, jnp.float32)

    (part,) = axis_sums(kept, got, "y")
    done = finish(center_two, [part] + from_others(part, "zl"))
    return level_one, place([done] + from_others(done, "y"), center_two)


def solution(mesh):
    fine = Mesh(mesh.devices.reshape(4, 4, 4, 2, 2), AXES)
    cent, pts = ("y", "zl"), ("x", "zh", "core")
    in_specs = (P(pts, None), P(cent, None), P(pts, None))
    out_specs = (P(cent + pts, None), P(pts, None))
    return jax.shard_map(shards, mesh=fine, in_specs=in_specs, out_specs=out_specs, check_vma=False)
```

```python
import functools

import jax
import jax.numpy as jnp
from jax import lax
from jax.experimental import pallas as pl
from jax.experimental.pallas import tpu as pltpu
from jax.sharding import Mesh
from jax.sharding import PartitionSpec as P

sharpness_coefficient = 100.0
AXES = ("y", "zl", "x", "zh", "core")
MIB = 1024 * 1024
VMEM = pl.BlockSpec(memory_space=pltpu.VMEM)
HBM = pl.BlockSpec(memory_space=pltpu.HBM)

def swapped(value, axis, mask=1):
    return lax.ppermute(value, axis, [(i, i ^ mask) for i in range(lax.axis_size(axis))])


OTHERS = {"y": (2, 1, 3), "x": (2, 1, 3), "zl": (3, 2, 1)}


def from_others(value, axis, masks=None):
    return [swapped(value, axis, k) for k in masks or OTHERS[axis]]


def kernel_call(body, name, flops, in_specs, out_specs, out_shape, vmem=12, **more):
    return pl.pallas_call(
        body,
        in_specs=in_specs,
        out_specs=out_specs,
        out_shape=out_shape,
        compiler_params=pltpu.CompilerParams(vmem_limit_bytes=vmem * MIB),
        cost_estimate=pl.CostEstimate(flops=flops, bytes_accessed=1024, transcendentals=0),
        name=name,
        **more,
    )


def f32(value):
    return value.astype(jnp.float32)


def bf16(value):
    return value.astype(jnp.bfloat16)


def shape(dims, dtype=jnp.bfloat16):
    return jax.ShapeDtypeStruct(dims, dtype)


def times_rows(left, right):
    return lax.dot_general(left, right, (((1,), (1,)), ((), ())), preferred_element_type=jnp.float32)


def merge(parts):
    peak = functools.reduce(jnp.maximum, [part[0:1] for part in parts])
    return peak, sum(part[1:2] * jnp.exp(part[0:1] - peak) for part in parts)


def normalize(values):
    return bf16(values * lax.rsqrt(jnp.mean(values * values, axis=-1, keepdims=True) + 1e-05))


def merge_kernel(count, *refs):
    peak, total = merge([ref[...] for ref in refs[:count]])
    refs[-1][0:1, :] = peak
    refs[-1][1:2, :] = total


def merge_stats(parts):
    return kernel_call(
        functools.partial(merge_kernel, len(parts)),
        "merge_stats",
        1_000_000,
        [VMEM] * len(parts),
        VMEM,
        shape(parts[0].shape, jnp.float32),
    )(*parts)


def powers_kernel(scale, step, center_ref, point_ref, power_ref, stat_ref):
    for start in range(0, point_ref.shape[0], step):
        columns = slice(start, start + step)
        raw = times_rows(center_ref[...], point_ref[columns, :])
        peak = jnp.max(raw, axis=0, keepdims=True)
        powers = jnp.exp((raw - peak) * scale)
        stat_ref[0:1, columns] = peak * scale
        stat_ref[1:2, columns] = jnp.sum(powers, axis=0, keepdims=True)
        power_ref[:, columns] = bf16(powers)


def level_one_powers(center, points, scale):
    held, depth = center.shape
    count = points.shape[0]
    return kernel_call(
        functools.partial(powers_kernel, scale, 512),
        "level_one_powers",
        2 * held * count * depth,
        [VMEM] * 2,
        [VMEM] * 2,
        [shape((held, count)), shape((2, count), jnp.float32)],
        vmem=20,
    )(center, points)


def sums_kernel(near, other_core, local_ref, *refs):
    stat_refs, power_ref, point_ref, out_ref = refs[:near], refs[near], refs[near + 1], refs[-1]
    nx, nh, _, owned, count = power_ref.shape
    peak, total = merge([ref[...] for ref in stat_refs])
    factor = jnp.exp(local_ref[0:1, :] - peak) / total
    core = lax.axis_index("core") ^ int(other_core)
    for k in range(nx):
        powers = power_ref[lax.axis_index("x") ^ k, :, core].reshape(nh * owned, count)
        weight = bf16(f32(powers) * factor)
        sums = jnp.dot(weight, point_ref[...], preferred_element_type=jnp.float32)
        out_ref[k] = sums.astype(out_ref.dtype).reshape(nh, owned, -1)


def level_one_sums(other_core, local, stats, powers, points, dtype):
    nx, nh, _, owned, count = powers.shape
    depth = points.shape[1]
    return kernel_call(
        functools.partial(sums_kernel, len(stats), other_core),
        "level_one_sums",
        2 * nx * nh * owned * count * depth,
        [VMEM] * (3 + len(stats)),
        VMEM,
        shape((nx, nh, owned, depth), dtype),
    )(local, *stats, powers, points)


def split_kernel(parts, kept_ref, got_ref, *refs):
    size = kept_ref.shape[0]
    for part in range(parts):
        hold_ref, *send_refs = refs[part * size : (part + 1) * size]
        hold_ref[...] = kept_ref[0, part] + f32(got_ref[0, part])
        for k, send_ref in enumerate(send_refs, 1):
            send_ref[...] = bf16(kept_ref[k, part] + f32(got_ref[k, part]))


def total_kernel(hold_ref, *refs):
    refs[-1][...] = bf16(hold_ref[...] + sum(f32(ref[...]) for ref in refs[:-1]))


def axis_sums(kept, got, axis):
    size, parts, *block = kept.shape
    outs = kernel_call(
        functools.partial(split_kernel, parts),
        "split",
        1_000_000,
        [VMEM] * 2,
        [VMEM] * (size * parts),
        ([shape(block, jnp.float32)] + [shape(block)] * (size - 1)) * parts,
    )(kept, got)
    sums = []
    for part in range(parts):
        hold, *sends = outs[part * size : (part + 1) * size]
        arrived = [swapped(sends[k - 1], axis, k) for k in OTHERS[axis]]
        sums.append(
            kernel_call(total_kernel, "total", 1_000_000, [VMEM] * size, VMEM, shape(block))(hold, *arrived)
        )
    return sums


def rows_kernel(half, part_ref, other_ref, center_hbm, row_ref, center_ref, sem):
    mine = center_hbm.at[lax.axis_index("x"), half, lax.axis_index("core")]
    copy = pltpu.make_async_copy(mine, center_ref, sem)
    copy.start()
    copy.wait()
    row_ref[...] = normalize(f32(part_ref[...]) + f32(other_ref[...]) + f32(center_ref[...]))


def new_rows(half, part, other, centers):
    return kernel_call(
        functools.partial(rows_kernel, half),
        "new_rows",
        1_000_000,
        [VMEM] * 2 + [HBM],
        VMEM,
        shape(part.shape),
        scratch_shapes=[pltpu.VMEM(part.shape, jnp.bfloat16), pltpu.SemaphoreType.DMA],
    )(part, other, centers)


def own_kernel(a_ref, b_ref, out_ref):
    out_ref[...] = jnp.where(lax.axis_index("zh") == 0, a_ref[...], b_ref[...])


def own_rows(a, b):
    return kernel_call(own_kernel, "own_rows", 1_000_000, [VMEM] * 2, VMEM, shape(a.shape))(a, b)


def powers_two_kernel(scale, ny, own_ref, other_ref, *refs):
    piece_refs, (row_ref, power_ref, stat_ref, center_ref) = refs[:-4], refs[-4:]
    held = own_ref.shape[0]
    block = held // ny
    for core, ref in enumerate((own_ref, other_ref)):
        for k in range(ny):
            place = pl.ds(pl.multiple_of((lax.axis_index("y") ^ k) * block, block), block)
            center_ref[core * held + k * block : core * held + (k + 1) * block, :] = ref[place, :]
    around = lax.axis_size("x")
    for i, ref in enumerate(piece_refs):
        size = ref.shape[0]
        mask = (0, *OTHERS["x"])[i % around]
        first = (lax.axis_index("x") ^ mask) * size + (i // around) * around * size
        row_ref[pl.ds(pl.multiple_of(first, size), size), :] = ref[...]
    raw = times_rows(center_ref[...], row_ref[...])
    peak = jnp.max(raw, axis=0, keepdims=True)
    powers = jnp.exp((raw - peak) * scale)
    stat_ref[0:1, :] = peak * scale
    stat_ref[1:2, :] = jnp.sum(powers, axis=0, keepdims=True)
    power_ref[...] = bf16(powers)


def level_two_powers(own, other, pieces, ny, scale):
    held, depth = own.shape
    count = sum(p.shape[0] for p in pieces)
    return kernel_call(
        functools.partial(powers_two_kernel, scale, ny),
        "level_two_powers",
        4 * held * count * depth,
        [VMEM] * (2 + len(pieces)),
        [VMEM] * 3,
        [shape((count, depth)), shape((2 * held, count)), shape((2, count), jnp.float32)],
        scratch_shapes=[pltpu.VMEM((2 * held, depth), jnp.bfloat16)],
    )(own, other, *pieces)


def sums_two_kernel(first, local_ref, power_ref, row_ref, *refs):
    stat_refs, out_ref = refs[:-1], refs[-1]
    peak, total = merge([ref[...] for ref in stat_refs])
    factor = jnp.exp(local_ref[0:1, :] - peak) / total
    held = power_ref.shape[0] // 2
    weight = bf16(f32(power_ref[first : first + held, :]) * factor)
    sums = jnp.dot(weight, row_ref[...], preferred_element_type=jnp.float32)
    out_ref[...] = sums.astype(out_ref.dtype).reshape(out_ref.shape)


def level_two_sums(other_core, local, stats, powers, rows, ny, dtype):
    held = powers.shape[0] // 2
    count, depth = rows.shape
    return kernel_call(
        functools.partial(sums_two_kernel, held if other_core else 0),
        "level_two_sums",
        2 * held * count * depth,
        [VMEM] * (3 + len(stats)),
        VMEM,
        shape((ny, 1, held // ny, depth), dtype),
    )(local, powers, rows, *stats)


def finish_kernel(center_ref, a_ref, b_ref, c_ref, d_ref, out_ref):
    size = a_ref.shape[0]
    values = (f32(a_ref[...]) + f32(b_ref[...])) + (f32(c_ref[...]) + f32(d_ref[...]))
    start = pl.multiple_of(lax.axis_index("y") * size, size)
    out_ref[...] = normalize(values + f32(center_ref[pl.ds(start, size), :]))


def finish(center, parts):
    return kernel_call(
        finish_kernel, "finish", 1_000_000, [VMEM] * 5, VMEM, shape(parts[0].shape)
    )(center, *parts)


def place_kernel(*refs):
    block_refs, out_ref, sems = refs[:-2], refs[-2], refs[-1]
    size = block_refs[0].shape[0]
    copies = []
    for i, (k, ref) in enumerate(zip((0, *OTHERS["y"]), block_refs)):
        rows = pl.ds(pl.multiple_of((lax.axis_index("y") ^ k) * size, size), size)
        copies.append(pltpu.make_async_copy(ref, out_ref.at[rows, :], sems.at[i]))
    for copy in copies:
        copy.start()
    for copy in copies:
        copy.wait()


def place(blocks, like):
    return kernel_call(
        place_kernel,
        "place",
        1_000_000,
        [VMEM] * len(blocks),
        HBM,
        shape(like.shape),
        scratch_shapes=[pltpu.SemaphoreType.DMA((len(blocks),))],
    )(*blocks)


def shards(points, center_one, center_two):
    held, depth = center_one.shape
    scale = sharpness_coefficient / depth
    ny, nl, nx, nh, nc = (lax.axis_size(a) for a in AXES)
    owned = held // (nx * nh * nc)

    powers, local = level_one_powers(center_one, points, scale)
    near = merge_stats([local] + from_others(local, "y"))
    powers = powers.reshape(nx, nh, nc, owned, -1)
    stats = [near] + from_others(near, "zl")
    sent = level_one_sums(True, local, stats, powers, points, jnp.bfloat16)
    got = swapped(sent, "core")
    kept = level_one_sums(False, local, stats, powers, points, jnp.float32)

    centers = center_one.reshape(nx, nh, nc, owned, depth)
    rows = []
    for half, part in enumerate(axis_sums(kept, got, "x")):
        rows.append(new_rows(half, part, swapped(part, "zh"), centers))
    level_one = own_rows(*rows)

    two_core = swapped(center_two, "core")
    pieces = [piece for half in rows for piece in [half] + from_others(half, "x")]
    rows, powers, local = level_two_powers(center_two, two_core, pieces, ny, scale)
    near = merge_stats([local] + from_others(local, "x"))
    stats = [near, swapped(near, "zh")]
    sent = level_two_sums(True, local, stats, powers, rows, ny, jnp.bfloat16)
    got = swapped(sent, "core")
    kept = level_two_sums(False, local, stats, powers, rows, ny, jnp.float32)

    (part,) = axis_sums(kept, got, "y")
    done = finish(center_two, [part] + from_others(part, "zl", (1, 2, 3)))
    return level_one, place([done] + from_others(done, "y"), center_two)


def solution(mesh):
    fine = Mesh(mesh.devices.reshape(4, 4, 4, 2, 2), AXES)
    cent, pts = ("y", "zl"), ("x", "zh", "core")
    in_specs = (P(pts, None), P(cent, None), P(pts, None))
    out_specs = (P(cent + pts, None), P(pts, None))
    return jax.shard_map(shards, mesh=fine, in_specs=in_specs, out_specs=out_specs, check_vma=False)
```

```python
import functools

import jax
import jax.numpy as jnp
from jax import lax
from jax.experimental import pallas as pl
from jax.experimental.pallas import tpu as pltpu
from jax.sharding import Mesh
from jax.sharding import PartitionSpec as P

sharpness_coefficient = 100.0
LOG2_E = 1.4426950408889634
AXES = ("y", "zl", "x", "zh", "core")
MIB = 1024 * 1024
VMEM = pl.BlockSpec(memory_space=pltpu.VMEM)
HBM = pl.BlockSpec(memory_space=pltpu.HBM)

def swapped(value, axis, mask=1):
    return lax.ppermute(value, axis, [(i, i ^ mask) for i in range(lax.axis_size(axis))])


OTHERS = {"y": (2, 1, 3), "x": (2, 1, 3), "zl": (3, 2, 1)}


def from_others(value, axis, masks=None):
    return [swapped(value, axis, k) for k in masks or OTHERS[axis]]


def kernel_call(body, name, flops, in_specs, out_specs, out_shape, vmem=12, **more):
    return pl.pallas_call(
        body,
        in_specs=in_specs,
        out_specs=out_specs,
        out_shape=out_shape,
        compiler_params=pltpu.CompilerParams(vmem_limit_bytes=vmem * MIB),
        cost_estimate=pl.CostEstimate(flops=flops, bytes_accessed=1024, transcendentals=0),
        name=name,
        **more,
    )


def f32(value):
    return value.astype(jnp.float32)


def bf16(value):
    return value.astype(jnp.bfloat16)


def shape(dims, dtype=jnp.bfloat16):
    return jax.ShapeDtypeStruct(dims, dtype)


def times_rows(left, right):
    return lax.dot_general(left, right, (((1,), (1,)), ((), ())), preferred_element_type=jnp.float32)


def merge(parts):
    peak = functools.reduce(jnp.maximum, [part[0:1] for part in parts])
    return peak, sum(part[1:2] * jnp.exp(part[0:1] - peak) for part in parts)


def normalize(values):
    return bf16(values * lax.rsqrt(jnp.mean(values * values, axis=-1, keepdims=True) + 1e-05))


def merge_kernel(count, *refs):
    peak, total = merge([ref[...] for ref in refs[:count]])
    refs[-1][0:1, :] = peak
    refs[-1][1:2, :] = total


def merge_stats(parts):
    return kernel_call(
        functools.partial(merge_kernel, len(parts)),
        "merge_stats",
        1_000_000,
        [VMEM] * len(parts),
        VMEM,
        shape(parts[0].shape, jnp.float32),
    )(*parts)


def powers_kernel(scale, step, center_ref, point_ref, power_ref, stat_ref):
    for start in range(0, point_ref.shape[0], step):
        columns = slice(start, start + step)
        raw = times_rows(center_ref[...], point_ref[columns, :])
        peak = jnp.max(raw, axis=0, keepdims=True)
        powers = jnp.exp2((raw - peak) * (scale * LOG2_E))
        stat_ref[0:1, columns] = peak * scale
        stat_ref[1:2, columns] = jnp.sum(powers, axis=0, keepdims=True)
        power_ref[:, columns] = bf16(powers)


def level_one_powers(center, points, scale):
    held, depth = center.shape
    count = points.shape[0]
    return kernel_call(
        functools.partial(powers_kernel, scale, 512),
        "level_one_powers",
        2 * held * count * depth,
        [VMEM] * 2,
        [VMEM] * 2,
        [shape((held, count)), shape((2, count), jnp.float32)],
        vmem=20,
    )(center, points)


def sums_kernel(near, other_core, half, local_ref, *refs):
    stat_refs, power_ref, point_ref, out_ref = refs[:near], refs[near], refs[near + 1], refs[-1]
    peak, total = merge([ref[...] for ref in stat_refs])
    factor = jnp.exp(local_ref[0:1, :] - peak) / total
    core = lax.axis_index("core") ^ int(other_core)
    blocks = [power_ref[lax.axis_index("x") ^ k, half, core] for k in range(power_ref.shape[0])]
    weight = bf16(f32(jnp.concatenate(blocks)) * factor)
    sums = jnp.dot(weight, point_ref[...], preferred_element_type=jnp.float32)
    out_ref[...] = sums.astype(out_ref.dtype).reshape(out_ref.shape)


def level_one_sums(other_core, half, local, stats, powers, points, dtype):
    nx, _, _, owned, count = powers.shape
    depth = points.shape[1]
    return kernel_call(
        functools.partial(sums_kernel, len(stats), other_core, half),
        "level_one_sums",
        2 * nx * owned * count * depth,
        [VMEM] * (3 + len(stats)),
        VMEM,
        shape((nx, 1, owned, depth), dtype),
    )(local, *stats, powers, points)


def split_kernel(parts, kept_ref, got_ref, *refs):
    size = kept_ref.shape[0]
    for part in range(parts):
        hold_ref, *send_refs = refs[part * size : (part + 1) * size]
        hold_ref[...] = kept_ref[0, part] + f32(got_ref[0, part])
        for k, send_ref in enumerate(send_refs, 1):
            send_ref[...] = bf16(kept_ref[k, part] + f32(got_ref[k, part]))


def total_kernel(hold_ref, *refs):
    refs[-1][...] = bf16(hold_ref[...] + sum(f32(ref[...]) for ref in refs[:-1]))


def axis_sums(kept, got, axis):
    size, parts, *block = kept.shape
    outs = kernel_call(
        functools.partial(split_kernel, parts),
        "split",
        1_000_000,
        [VMEM] * 2,
        [VMEM] * (size * parts),
        ([shape(block, jnp.float32)] + [shape(block)] * (size - 1)) * parts,
    )(kept, got)
    sums = []
    for part in range(parts):
        hold, *sends = outs[part * size : (part + 1) * size]
        arrived = [swapped(sends[k - 1], axis, k) for k in OTHERS[axis]]
        sums.append(
            kernel_call(total_kernel, "total", 1_000_000, [VMEM] * size, VMEM, shape(block))(hold, *arrived)
        )
    return sums


def rows_kernel(half, part_ref, other_ref, center_hbm, row_ref, center_ref, sem):
    mine = center_hbm.at[lax.axis_index("x"), half, lax.axis_index("core")]
    copy = pltpu.make_async_copy(mine, center_ref, sem)
    copy.start()
    copy.wait()
    row_ref[...] = normalize(f32(part_ref[...]) + f32(other_ref[...]) + f32(center_ref[...]))


def new_rows(half, part, other, centers):
    return kernel_call(
        functools.partial(rows_kernel, half),
        "new_rows",
        1_000_000,
        [VMEM] * 2 + [HBM],
        VMEM,
        shape(part.shape),
        scratch_shapes=[pltpu.VMEM(part.shape, jnp.bfloat16), pltpu.SemaphoreType.DMA],
    )(part, other, centers)


def own_kernel(a_ref, b_ref, out_ref):
    out_ref[...] = jnp.where(lax.axis_index("zh") == 0, a_ref[...], b_ref[...])


def own_rows(a, b):
    return kernel_call(own_kernel, "own_rows", 1_000_000, [VMEM] * 2, VMEM, shape(a.shape))(a, b)


def powers_two_kernel(scale, ny, own_ref, other_ref, *refs):
    piece_refs, (row_ref, power_ref, stat_ref, center_ref) = refs[:-4], refs[-4:]
    held = own_ref.shape[0]
    block = held // ny
    for core, ref in enumerate((own_ref, other_ref)):
        for k in range(ny):
            place = pl.ds(pl.multiple_of((lax.axis_index("y") ^ k) * block, block), block)
            center_ref[core * held + k * block : core * held + (k + 1) * block, :] = ref[place, :]
    around = lax.axis_size("x")
    for i, ref in enumerate(piece_refs):
        size = ref.shape[0]
        mask = (0, *OTHERS["x"])[i % around]
        first = (lax.axis_index("x") ^ mask) * size + (i // around) * around * size
        row_ref[pl.ds(pl.multiple_of(first, size), size), :] = ref[...]
    raw = times_rows(center_ref[...], row_ref[...])
    peak = jnp.max(raw, axis=0, keepdims=True)
    powers = jnp.exp((raw - peak) * scale)
    stat_ref[0:1, :] = peak * scale
    stat_ref[1:2, :] = jnp.sum(powers, axis=0, keepdims=True)
    power_ref[...] = bf16(powers)


def level_two_powers(own, other, pieces, ny, scale):
    held, depth = own.shape
    count = sum(p.shape[0] for p in pieces)
    return kernel_call(
        functools.partial(powers_two_kernel, scale, ny),
        "level_two_powers",
        4 * held * count * depth,
        [VMEM] * (2 + len(pieces)),
        [VMEM] * 3,
        [shape((count, depth)), shape((2 * held, count)), shape((2, count), jnp.float32)],
        scratch_shapes=[pltpu.VMEM((2 * held, depth), jnp.bfloat16)],
    )(own, other, *pieces)


def sums_two_kernel(first, local_ref, power_ref, row_ref, *refs):
    stat_refs, out_ref = refs[:-1], refs[-1]
    peak, total = merge([ref[...] for ref in stat_refs])
    factor = jnp.exp(local_ref[0:1, :] - peak) / total
    held = power_ref.shape[0] // 2
    weight = bf16(f32(power_ref[first : first + held, :]) * factor)
    sums = jnp.dot(weight, row_ref[...], preferred_element_type=jnp.float32)
    out_ref[...] = sums.astype(out_ref.dtype).reshape(out_ref.shape)


def level_two_sums(other_core, local, stats, powers, rows, ny, dtype):
    held = powers.shape[0] // 2
    count, depth = rows.shape
    return kernel_call(
        functools.partial(sums_two_kernel, held if other_core else 0),
        "level_two_sums",
        2 * held * count * depth,
        [VMEM] * (3 + len(stats)),
        VMEM,
        shape((ny, 1, held // ny, depth), dtype),
    )(local, powers, rows, *stats)


def finish_kernel(center_ref, a_ref, b_ref, c_ref, d_ref, out_ref):
    size = a_ref.shape[0]
    values = (f32(a_ref[...]) + f32(b_ref[...])) + (f32(c_ref[...]) + f32(d_ref[...]))
    start = pl.multiple_of(lax.axis_index("y") * size, size)
    out_ref[...] = normalize(values + f32(center_ref[pl.ds(start, size), :]))


def finish(center, parts):
    return kernel_call(
        finish_kernel, "finish", 1_000_000, [VMEM] * 5, VMEM, shape(parts[0].shape)
    )(center, *parts)


def place_kernel(*refs):
    block_refs, out_ref, sems = refs[:-2], refs[-2], refs[-1]
    size = block_refs[0].shape[0]
    copies = []
    for i, (k, ref) in enumerate(zip((0, *OTHERS["y"]), block_refs)):
        rows = pl.ds(pl.multiple_of((lax.axis_index("y") ^ k) * size, size), size)
        copies.append(pltpu.make_async_copy(ref, out_ref.at[rows, :], sems.at[i]))
    for copy in copies:
        copy.start()
    for copy in copies:
        copy.wait()


def place(blocks, like):
    return kernel_call(
        place_kernel,
        "place",
        1_000_000,
        [VMEM] * len(blocks),
        HBM,
        shape(like.shape),
        scratch_shapes=[pltpu.SemaphoreType.DMA((len(blocks),))],
    )(*blocks)


def shards(points, center_one, center_two):
    held, depth = center_one.shape
    scale = sharpness_coefficient / depth
    ny, nl, nx, nh, nc = (lax.axis_size(a) for a in AXES)
    owned = held // (nx * nh * nc)

    powers, local = level_one_powers(center_one, points, scale)
    near = merge_stats([local] + from_others(local, "y"))
    powers = powers.reshape(nx, nh, nc, owned, -1)
    stats = [near] + from_others(near, "zl")

    centers = center_one.reshape(nx, nh, nc, owned, depth)
    rows = []
    for half in range(nh):
        sent = level_one_sums(True, half, local, stats, powers, points, jnp.bfloat16)
        got = swapped(sent, "core")
        kept = level_one_sums(False, half, local, stats, powers, points, jnp.float32)
        (part,) = axis_sums(kept, got, "x")
        rows.append(new_rows(half, part, swapped(part, "zh"), centers))
    level_one = own_rows(*rows)

    two_core = swapped(center_two, "core")
    pieces = [piece for half in rows for piece in [half] + from_others(half, "x")]
    rows, powers, local = level_two_powers(center_two, two_core, pieces, ny, scale)
    near = merge_stats([local] + from_others(local, "x"))
    stats = [near, swapped(near, "zh")]
    sent = level_two_sums(True, local, stats, powers, rows, ny, jnp.bfloat16)
    got = swapped(sent, "core")
    kept = level_two_sums(False, local, stats, powers, rows, ny, jnp.float32)

    (part,) = axis_sums(kept, got, "y")
    done = finish(center_two, [part] + from_others(part, "zl", (1, 2, 3)))
    return level_one, place([done] + from_others(done, "y"), center_two)


def solution(mesh):
    fine = Mesh(mesh.devices.reshape(4, 4, 4, 2, 2), AXES)
    cent, pts = ("y", "zl"), ("x", "zh", "core")
    in_specs = (P(pts, None), P(cent, None), P(pts, None))
    out_specs = (P(cent + pts, None), P(pts, None))
    return jax.shard_map(shards, mesh=fine, in_specs=in_specs, out_specs=out_specs, check_vma=False)
```

```python
import functools

import jax
import jax.numpy as jnp
from jax import lax
from jax.experimental import pallas as pl
from jax.experimental.pallas import tpu as pltpu
from jax.sharding import Mesh
from jax.sharding import PartitionSpec as P

sharpness_coefficient = 100.0
LOG2_E = 1.4426950408889634
AXES = ("y", "zl", "x", "zh", "core")
MIB = 1024 * 1024
VMEM = pl.BlockSpec(memory_space=pltpu.VMEM)
HBM = pl.BlockSpec(memory_space=pltpu.HBM)

def swapped(value, axis, mask=1):
    return lax.ppermute(value, axis, [(i, i ^ mask) for i in range(lax.axis_size(axis))])


OTHERS = {"y": (2, 1, 3), "x": (2, 1, 3), "zl": (3, 2, 1)}


def from_others(value, axis, masks=None):
    return [swapped(value, axis, k) for k in masks or OTHERS[axis]]


def kernel_call(body, name, flops, in_specs, out_specs, out_shape, vmem=12, **more):
    return pl.pallas_call(
        body,
        in_specs=in_specs,
        out_specs=out_specs,
        out_shape=out_shape,
        compiler_params=pltpu.CompilerParams(vmem_limit_bytes=vmem * MIB),
        cost_estimate=pl.CostEstimate(flops=flops, bytes_accessed=1024, transcendentals=0),
        name=name,
        **more,
    )


def f32(value):
    return value.astype(jnp.float32)


def bf16(value):
    return value.astype(jnp.bfloat16)


def shape(dims, dtype=jnp.bfloat16):
    return jax.ShapeDtypeStruct(dims, dtype)


def times_rows(left, right):
    return lax.dot_general(left, right, (((1,), (1,)), ((), ())), preferred_element_type=jnp.float32)


def merge(parts):
    peak = functools.reduce(jnp.maximum, [part[0:1] for part in parts])
    return peak, sum(part[1:2] * jnp.exp(part[0:1] - peak) for part in parts)


def normalize(values):
    return bf16(values * lax.rsqrt(jnp.mean(values * values, axis=-1, keepdims=True) + 1e-05))


def merge_kernel(count, *refs):
    peak, total = merge([ref[...] for ref in refs[:count]])
    refs[-1][0:1, :] = peak
    refs[-1][1:2, :] = total


def merge_stats(parts):
    return kernel_call(
        functools.partial(merge_kernel, len(parts)),
        "merge_stats",
        1_000_000,
        [VMEM] * len(parts),
        VMEM,
        shape(parts[0].shape, jnp.float32),
    )(*parts)


def powers_kernel(scale, step, center_ref, point_ref, power_ref, stat_ref):
    for start in range(0, point_ref.shape[0], step):
        columns = slice(start, start + step)
        raw = times_rows(center_ref[...], point_ref[columns, :])
        peak = jnp.max(raw, axis=0, keepdims=True)
        powers = jnp.exp2((raw - peak) * (scale * LOG2_E))
        stat_ref[0:1, columns] = peak * scale
        stat_ref[1:2, columns] = jnp.sum(powers, axis=0, keepdims=True)
        power_ref[:, columns] = bf16(powers)


def level_one_powers(center, points, scale):
    held, depth = center.shape
    count = points.shape[0]
    return kernel_call(
        functools.partial(powers_kernel, scale, 512),
        "level_one_powers",
        2 * held * count * depth,
        [VMEM] * 2,
        [VMEM] * 2,
        [shape((held, count)), shape((2, count), jnp.float32)],
        vmem=20,
    )(center, points)


def sums_kernel(near, other_core, half, local_ref, *refs):
    stat_refs, power_ref, point_ref, out_ref = refs[:near], refs[near], refs[near + 1], refs[-1]
    peak, total = merge([ref[...] for ref in stat_refs])
    factor = jnp.exp(local_ref[0:1, :] - peak) / total
    core = lax.axis_index("core") ^ int(other_core)
    blocks = [power_ref[lax.axis_index("x") ^ k, half, core] for k in range(power_ref.shape[0])]
    weight = bf16(f32(jnp.concatenate(blocks)) * factor)
    sums = jnp.dot(weight, point_ref[...], preferred_element_type=jnp.float32)
    out_ref[...] = sums.astype(out_ref.dtype).reshape(out_ref.shape)


def level_one_sums(other_core, half, local, stats, powers, points, dtype):
    nx, _, _, owned, count = powers.shape
    depth = points.shape[1]
    return kernel_call(
        functools.partial(sums_kernel, len(stats), other_core, half),
        "level_one_sums",
        2 * nx * owned * count * depth,
        [VMEM] * (3 + len(stats)),
        VMEM,
        shape((nx, 1, owned, depth), dtype),
    )(local, *stats, powers, points)


def split_kernel(parts, kept_ref, got_ref, *refs):
    size = kept_ref.shape[0]
    for part in range(parts):
        hold_ref, *send_refs = refs[part * size : (part + 1) * size]
        hold_ref[...] = kept_ref[0, part] + f32(got_ref[0, part])
        for k, send_ref in enumerate(send_refs, 1):
            send_ref[...] = bf16(kept_ref[k, part] + f32(got_ref[k, part]))


def total_kernel(hold_ref, *refs):
    refs[-1][...] = bf16(hold_ref[...] + sum(f32(ref[...]) for ref in refs[:-1]))


def axis_sums(kept, got, axis):
    size, parts, *block = kept.shape
    outs = kernel_call(
        functools.partial(split_kernel, parts),
        "split",
        1_000_000,
        [VMEM] * 2,
        [VMEM] * (size * parts),
        ([shape(block, jnp.float32)] + [shape(block)] * (size - 1)) * parts,
    )(kept, got)
    sums = []
    for part in range(parts):
        hold, *sends = outs[part * size : (part + 1) * size]
        arrived = [swapped(sends[k - 1], axis, k) for k in OTHERS[axis]]
        sums.append(
            kernel_call(total_kernel, "total", 1_000_000, [VMEM] * size, VMEM, shape(block))(hold, *arrived)
        )
    return sums


def rows_kernel(half, part_ref, other_ref, center_hbm, row_ref, center_ref, sem):
    mine = center_hbm.at[lax.axis_index("x"), half, lax.axis_index("core")]
    copy = pltpu.make_async_copy(mine, center_ref, sem)
    copy.start()
    copy.wait()
    row_ref[...] = normalize(f32(part_ref[...]) + f32(other_ref[...]) + f32(center_ref[...]))


def new_rows(half, part, other, centers):
    return kernel_call(
        functools.partial(rows_kernel, half),
        "new_rows",
        1_000_000,
        [VMEM] * 2 + [HBM],
        VMEM,
        shape(part.shape),
        scratch_shapes=[pltpu.VMEM(part.shape, jnp.bfloat16), pltpu.SemaphoreType.DMA],
    )(part, other, centers)


def own_kernel(a_ref, b_ref, out_ref):
    out_ref[...] = jnp.where(lax.axis_index("zh") == 0, a_ref[...], b_ref[...])


def own_rows(a, b):
    return kernel_call(own_kernel, "own_rows", 1_000_000, [VMEM] * 2, VMEM, shape(a.shape))(a, b)


def powers_two_kernel(scale, ny, own_ref, other_ref, *refs):
    piece_refs, (row_ref, power_ref, stat_ref, center_ref) = refs[:-4], refs[-4:]
    held = own_ref.shape[0]
    block = held // ny
    for core, ref in enumerate((own_ref, other_ref)):
        for k in range(ny):
            place = pl.ds(pl.multiple_of((lax.axis_index("y") ^ k) * block, block), block)
            center_ref[core * held + k * block : core * held + (k + 1) * block, :] = ref[place, :]
    around = lax.axis_size("x")
    for i, ref in enumerate(piece_refs):
        size = ref.shape[0]
        mask = (0, *OTHERS["x"])[i % around]
        first = (lax.axis_index("x") ^ mask) * size + (i // around) * around * size
        row_ref[pl.ds(pl.multiple_of(first, size), size), :] = ref[...]
    raw = times_rows(center_ref[...], row_ref[...])
    peak = jnp.max(raw, axis=0, keepdims=True)
    powers = jnp.exp2((raw - peak) * (scale * LOG2_E))
    stat_ref[0:1, :] = peak * scale
    stat_ref[1:2, :] = jnp.sum(powers, axis=0, keepdims=True)
    power_ref[...] = bf16(powers)


def level_two_powers(own, other, pieces, ny, scale):
    held, depth = own.shape
    count = sum(p.shape[0] for p in pieces)
    return kernel_call(
        functools.partial(powers_two_kernel, scale, ny),
        "level_two_powers",
        4 * held * count * depth,
        [VMEM] * (2 + len(pieces)),
        [VMEM] * 3,
        [shape((count, depth)), shape((2 * held, count)), shape((2, count), jnp.float32)],
        scratch_shapes=[pltpu.VMEM((2 * held, depth), jnp.bfloat16)],
    )(own, other, *pieces)


def sums_two_kernel(first, local_ref, power_ref, row_ref, *refs):
    stat_refs, out_ref = refs[:-1], refs[-1]
    peak, total = merge([ref[...] for ref in stat_refs])
    factor = jnp.exp(local_ref[0:1, :] - peak) / total
    held = power_ref.shape[0] // 2
    weight = bf16(f32(power_ref[first : first + held, :]) * factor)
    sums = jnp.dot(weight, row_ref[...], preferred_element_type=jnp.float32)
    out_ref[...] = sums.astype(out_ref.dtype).reshape(out_ref.shape)


def level_two_sums(other_core, local, stats, powers, rows, ny, dtype):
    held = powers.shape[0] // 2
    count, depth = rows.shape
    return kernel_call(
        functools.partial(sums_two_kernel, held if other_core else 0),
        "level_two_sums",
        2 * held * count * depth,
        [VMEM] * (3 + len(stats)),
        VMEM,
        shape((ny, 1, held // ny, depth), dtype),
    )(local, powers, rows, *stats)


def finish_kernel(center_ref, a_ref, b_ref, c_ref, d_ref, out_ref):
    size = a_ref.shape[0]
    values = (f32(a_ref[...]) + f32(b_ref[...])) + (f32(c_ref[...]) + f32(d_ref[...]))
    start = pl.multiple_of(lax.axis_index("y") * size, size)
    out_ref[...] = normalize(values + f32(center_ref[pl.ds(start, size), :]))


def finish(center, parts):
    return kernel_call(
        finish_kernel, "finish", 1_000_000, [VMEM] * 5, VMEM, shape(parts[0].shape)
    )(center, *parts)


def place_kernel(*refs):
    block_refs, out_ref, sems = refs[:-2], refs[-2], refs[-1]
    size = block_refs[0].shape[0]
    copies = []
    for i, (k, ref) in enumerate(zip((0, *OTHERS["y"]), block_refs)):
        rows = pl.ds(pl.multiple_of((lax.axis_index("y") ^ k) * size, size), size)
        copies.append(pltpu.make_async_copy(ref, out_ref.at[rows, :], sems.at[i]))
    for copy in copies:
        copy.start()
    for copy in copies:
        copy.wait()


def place(blocks, like):
    return kernel_call(
        place_kernel,
        "place",
        1_000_000,
        [VMEM] * len(blocks),
        HBM,
        shape(like.shape),
        scratch_shapes=[pltpu.SemaphoreType.DMA((len(blocks),))],
    )(*blocks)


def shards(points, center_one, center_two):
    held, depth = center_one.shape
    scale = sharpness_coefficient / depth
    ny, nl, nx, nh, nc = (lax.axis_size(a) for a in AXES)
    owned = held // (nx * nh * nc)

    powers, local = level_one_powers(center_one, points, scale)
    near = merge_stats([local] + from_others(local, "y"))
    powers = powers.reshape(nx, nh, nc, owned, -1)
    stats = [near] + from_others(near, "zl")

    centers = center_one.reshape(nx, nh, nc, owned, depth)
    rows = []
    for half in range(nh):
        sent = level_one_sums(True, half, local, stats, powers, points, jnp.bfloat16)
        got = swapped(sent, "core")
        kept = level_one_sums(False, half, local, stats, powers, points, jnp.float32)
        (part,) = axis_sums(kept, got, "x")
        rows.append(new_rows(half, part, swapped(part, "zh"), centers))
    level_one = own_rows(*rows)

    two_core = swapped(center_two, "core")
    pieces = [piece for half in rows for piece in [half] + from_others(half, "x")]
    rows, powers, local = level_two_powers(center_two, two_core, pieces, ny, scale)
    near = merge_stats([local, swapped(local, "zh")])
    stats = [near] + from_others(near, "x")
    sent = level_two_sums(True, local, stats, powers, rows, ny, jnp.bfloat16)
    got = swapped(sent, "core")
    kept = level_two_sums(False, local, stats, powers, rows, ny, jnp.float32)

    (part,) = axis_sums(kept, got, "y")
    done = finish(center_two, [part] + from_others(part, "zl", (1, 2, 3)))
    return level_one, place([done] + from_others(done, "y"), center_two)


def solution(mesh):
    fine = Mesh(mesh.devices.reshape(4, 4, 4, 2, 2), AXES)
    cent, pts = ("y", "zl"), ("x", "zh", "core")
    in_specs = (P(pts, None), P(cent, None), P(pts, None))
    out_specs = (P(cent + pts, None), P(pts, None))
    return jax.shard_map(shards, mesh=fine, in_specs=in_specs, out_specs=out_specs, check_vma=False)
```

```python
import functools

import jax
import jax.numpy as jnp
from jax import lax
from jax.experimental import pallas as pl
from jax.experimental.pallas import tpu as pltpu
from jax.sharding import Mesh
from jax.sharding import PartitionSpec as P

sharpness_coefficient = 100.0
LOG2_E = 1.4426950408889634
AXES = ("y", "zl", "x", "zh", "core")
MIB = 1024 * 1024
VMEM = pl.BlockSpec(memory_space=pltpu.VMEM)
HBM = pl.BlockSpec(memory_space=pltpu.HBM)

def swapped(value, axis, mask=1):
    return lax.ppermute(value, axis, [(i, i ^ mask) for i in range(lax.axis_size(axis))])


OTHERS = {"y": (2, 1, 3), "x": (2, 1, 3), "zl": (3, 2, 1)}


def from_others(value, axis, masks=None):
    return [swapped(value, axis, k) for k in masks or OTHERS[axis]]


def kernel_call(body, name, flops, in_specs, out_specs, out_shape, vmem=12, **more):
    return pl.pallas_call(
        body,
        in_specs=in_specs,
        out_specs=out_specs,
        out_shape=out_shape,
        compiler_params=pltpu.CompilerParams(vmem_limit_bytes=vmem * MIB),
        cost_estimate=pl.CostEstimate(flops=flops, bytes_accessed=1024, transcendentals=0),
        name=name,
        **more,
    )


def f32(value):
    return value.astype(jnp.float32)


def bf16(value):
    return value.astype(jnp.bfloat16)


def shape(dims, dtype=jnp.bfloat16):
    return jax.ShapeDtypeStruct(dims, dtype)


def times_rows(left, right):
    return lax.dot_general(left, right, (((1,), (1,)), ((), ())), preferred_element_type=jnp.float32)


def merge(parts):
    peak = functools.reduce(jnp.maximum, [part[0:1] for part in parts])
    return peak, sum(part[1:2] * jnp.exp(part[0:1] - peak) for part in parts)


def normalize(values):
    return bf16(values * lax.rsqrt(jnp.mean(values * values, axis=-1, keepdims=True) + 1e-05))


def merge_kernel(count, *refs):
    peak, total = merge([ref[...] for ref in refs[:count]])
    refs[-1][0:1, :] = peak
    refs[-1][1:2, :] = total


def merge_stats(parts):
    return kernel_call(
        functools.partial(merge_kernel, len(parts)),
        "merge_stats",
        1_000_000,
        [VMEM] * len(parts),
        VMEM,
        shape(parts[0].shape, jnp.float32),
    )(*parts)


def powers_kernel(scale, step, center_ref, point_ref, power_ref, stat_ref):
    for start in range(0, point_ref.shape[0], step):
        columns = slice(start, start + step)
        raw = times_rows(center_ref[...], point_ref[columns, :])
        peak = jnp.max(raw, axis=0, keepdims=True)
        powers = jnp.exp2((raw - peak) * (scale * LOG2_E))
        stat_ref[0:1, columns] = peak * scale
        stat_ref[1:2, columns] = jnp.sum(powers, axis=0, keepdims=True)
        power_ref[:, columns] = bf16(powers)


def level_one_powers(center, points, scale):
    held, depth = center.shape
    count = points.shape[0]
    return kernel_call(
        functools.partial(powers_kernel, scale, 1024),
        "level_one_powers",
        2 * held * count * depth,
        [VMEM] * 2,
        [VMEM] * 2,
        [shape((held, count)), shape((2, count), jnp.float32)],
        vmem=28,
    )(center, points)


def sums_kernel(near, other_core, half, local_ref, *refs):
    stat_refs, power_ref, point_ref, out_ref = refs[:near], refs[near], refs[near + 1], refs[-1]
    peak, total = merge([ref[...] for ref in stat_refs])
    factor = jnp.exp(local_ref[0:1, :] - peak) / total
    core = lax.axis_index("core") ^ int(other_core)
    blocks = [power_ref[lax.axis_index("x") ^ k, half, core] for k in range(power_ref.shape[0])]
    weight = bf16(f32(jnp.concatenate(blocks)) * factor)
    sums = jnp.dot(weight, point_ref[...], preferred_element_type=jnp.float32)
    out_ref[...] = sums.astype(out_ref.dtype).reshape(out_ref.shape)


def level_one_sums(other_core, half, local, stats, powers, points, dtype):
    nx, _, _, owned, count = powers.shape
    depth = points.shape[1]
    return kernel_call(
        functools.partial(sums_kernel, len(stats), other_core, half),
        "level_one_sums",
        2 * nx * owned * count * depth,
        [VMEM] * (3 + len(stats)),
        VMEM,
        shape((nx, 1, owned, depth), dtype),
    )(local, *stats, powers, points)


def split_kernel(parts, kept_ref, got_ref, *refs):
    size = kept_ref.shape[0]
    for part in range(parts):
        hold_ref, *send_refs = refs[part * size : (part + 1) * size]
        hold_ref[...] = kept_ref[0, part] + f32(got_ref[0, part])
        for k, send_ref in enumerate(send_refs, 1):
            send_ref[...] = bf16(kept_ref[k, part] + f32(got_ref[k, part]))


def total_kernel(hold_ref, *refs):
    refs[-1][...] = bf16(hold_ref[...] + sum(f32(ref[...]) for ref in refs[:-1]))


def axis_sums(kept, got, axis):
    size, parts, *block = kept.shape
    outs = kernel_call(
        functools.partial(split_kernel, parts),
        "split",
        1_000_000,
        [VMEM] * 2,
        [VMEM] * (size * parts),
        ([shape(block, jnp.float32)] + [shape(block)] * (size - 1)) * parts,
    )(kept, got)
    sums = []
    for part in range(parts):
        hold, *sends = outs[part * size : (part + 1) * size]
        arrived = [swapped(sends[k - 1], axis, k) for k in OTHERS[axis]]
        sums.append(
            kernel_call(total_kernel, "total", 1_000_000, [VMEM] * size, VMEM, shape(block))(hold, *arrived)
        )
    return sums


def rows_kernel(half, part_ref, other_ref, center_hbm, row_ref, center_ref, sem):
    mine = center_hbm.at[lax.axis_index("x"), half, lax.axis_index("core")]
    copy = pltpu.make_async_copy(mine, center_ref, sem)
    copy.start()
    copy.wait()
    row_ref[...] = normalize(f32(part_ref[...]) + f32(other_ref[...]) + f32(center_ref[...]))


def new_rows(half, part, other, centers):
    return kernel_call(
        functools.partial(rows_kernel, half),
        "new_rows",
        1_000_000,
        [VMEM] * 2 + [HBM],
        VMEM,
        shape(part.shape),
        scratch_shapes=[pltpu.VMEM(part.shape, jnp.bfloat16), pltpu.SemaphoreType.DMA],
    )(part, other, centers)


def own_kernel(a_ref, b_ref, out_ref):
    out_ref[...] = jnp.where(lax.axis_index("zh") == 0, a_ref[...], b_ref[...])


def own_rows(a, b):
    return kernel_call(own_kernel, "own_rows", 1_000_000, [VMEM] * 2, VMEM, shape(a.shape))(a, b)


def powers_two_kernel(scale, ny, own_ref, other_ref, *refs):
    piece_refs, (row_ref, power_ref, stat_ref, center_ref) = refs[:-4], refs[-4:]
    held = own_ref.shape[0]
    block = held // ny
    for core, ref in enumerate((own_ref, other_ref)):
        for k in range(ny):
            place = pl.ds(pl.multiple_of((lax.axis_index("y") ^ k) * block, block), block)
            center_ref[core * held + k * block : core * held + (k + 1) * block, :] = ref[place, :]
    around = lax.axis_size("x")
    for i, ref in enumerate(piece_refs):
        size = ref.shape[0]
        mask = (0, *OTHERS["x"])[i % around]
        first = (lax.axis_index("x") ^ mask) * size + (i // around) * around * size
        row_ref[pl.ds(pl.multiple_of(first, size), size), :] = ref[...]
    raw = times_rows(center_ref[...], row_ref[...])
    peak = jnp.max(raw, axis=0, keepdims=True)
    powers = jnp.exp((raw - peak) * scale)
    stat_ref[0:1, :] = peak * scale
    stat_ref[1:2, :] = jnp.sum(powers, axis=0, keepdims=True)
    power_ref[...] = bf16(powers)


def level_two_powers(own, other, pieces, ny, scale):
    held, depth = own.shape
    count = sum(p.shape[0] for p in pieces)
    return kernel_call(
        functools.partial(powers_two_kernel, scale, ny),
        "level_two_powers",
        4 * held * count * depth,
        [VMEM] * (2 + len(pieces)),
        [VMEM] * 3,
        [shape((count, depth)), shape((2 * held, count)), shape((2, count), jnp.float32)],
        scratch_shapes=[pltpu.VMEM((2 * held, depth), jnp.bfloat16)],
    )(own, other, *pieces)


def sums_two_kernel(first, local_ref, power_ref, row_ref, *refs):
    stat_refs, out_ref = refs[:-1], refs[-1]
    peak, total = merge([ref[...] for ref in stat_refs])
    factor = jnp.exp(local_ref[0:1, :] - peak) / total
    held = power_ref.shape[0] // 2
    weight = bf16(f32(power_ref[first : first + held, :]) * factor)
    sums = jnp.dot(weight, row_ref[...], preferred_element_type=jnp.float32)
    out_ref[...] = sums.astype(out_ref.dtype).reshape(out_ref.shape)


def level_two_sums(other_core, local, stats, powers, rows, ny, dtype):
    held = powers.shape[0] // 2
    count, depth = rows.shape
    return kernel_call(
        functools.partial(sums_two_kernel, held if other_core else 0),
        "level_two_sums",
        2 * held * count * depth,
        [VMEM] * (3 + len(stats)),
        VMEM,
        shape((ny, 1, held // ny, depth), dtype),
    )(local, powers, rows, *stats)


def finish_kernel(center_ref, a_ref, b_ref, c_ref, d_ref, out_ref):
    size = a_ref.shape[0]
    values = (f32(a_ref[...]) + f32(b_ref[...])) + (f32(c_ref[...]) + f32(d_ref[...]))
    start = pl.multiple_of(lax.axis_index("y") * size, size)
    out_ref[...] = normalize(values + f32(center_ref[pl.ds(start, size), :]))


def finish(center, parts):
    return kernel_call(
        finish_kernel, "finish", 1_000_000, [VMEM] * 5, VMEM, shape(parts[0].shape)
    )(center, *parts)


def place_kernel(*refs):
    block_refs, out_ref, sems = refs[:-2], refs[-2], refs[-1]
    size = block_refs[0].shape[0]
    copies = []
    for i, (k, ref) in enumerate(zip((0, *OTHERS["y"]), block_refs)):
        rows = pl.ds(pl.multiple_of((lax.axis_index("y") ^ k) * size, size), size)
        copies.append(pltpu.make_async_copy(ref, out_ref.at[rows, :], sems.at[i]))
    for copy in copies:
        copy.start()
    for copy in copies:
        copy.wait()


def place(blocks, like):
    return kernel_call(
        place_kernel,
        "place",
        1_000_000,
        [VMEM] * len(blocks),
        HBM,
        shape(like.shape),
        scratch_shapes=[pltpu.SemaphoreType.DMA((len(blocks),))],
    )(*blocks)


def shards(points, center_one, center_two):
    held, depth = center_one.shape
    scale = sharpness_coefficient / depth
    ny, nl, nx, nh, nc = (lax.axis_size(a) for a in AXES)
    owned = held // (nx * nh * nc)

    powers, local = level_one_powers(center_one, points, scale)
    near = merge_stats([local] + from_others(local, "y"))
    powers = powers.reshape(nx, nh, nc, owned, -1)
    stats = [near] + from_others(near, "zl")

    centers = center_one.reshape(nx, nh, nc, owned, depth)
    rows = []
    for half in range(nh):
        sent = level_one_sums(True, half, local, stats, powers, points, jnp.bfloat16)
        got = swapped(sent, "core")
        kept = level_one_sums(False, half, local, stats, powers, points, jnp.float32)
        (part,) = axis_sums(kept, got, "x")
        rows.append(new_rows(half, part, swapped(part, "zh"), centers))
    level_one = own_rows(*rows)

    two_core = swapped(center_two, "core")
    pieces = [piece for half in rows for piece in [half] + from_others(half, "x")]
    rows, powers, local = level_two_powers(center_two, two_core, pieces, ny, scale)
    near = merge_stats([local] + from_others(local, "x"))
    stats = [near, swapped(near, "zh")]
    sent = level_two_sums(True, local, stats, powers, rows, ny, jnp.bfloat16)
    got = swapped(sent, "core")
    kept = level_two_sums(False, local, stats, powers, rows, ny, jnp.float32)

    (part,) = axis_sums(kept, got, "y")
    done = finish(center_two, [part] + from_others(part, "zl", (1, 2, 3)))
    return level_one, place([done] + from_others(done, "y"), center_two)


def solution(mesh):
    fine = Mesh(mesh.devices.reshape(4, 4, 4, 2, 2), AXES)
    cent, pts = ("y", "zl"), ("x", "zh", "core")
    in_specs = (P(pts, None), P(cent, None), P(pts, None))
    out_specs = (P(cent + pts, None), P(pts, None))
    return jax.shard_map(shards, mesh=fine, in_specs=in_specs, out_specs=out_specs, check_vma=False)
```
